32 devices in a mesh: pb: 8 (over z, y), col: 4 (over x, core).
Axes of the slice: x: 2, y: 2, z: 4, core: 2. Of those that a mesh axis runs over, the one named last changes fastest.
Arguments:
- queries: bfloat16 [12288, 1024], P(('pb', 'col')), may hold values from -5 to 18
- groups: bfloat16 [1024, 1024], P(('pb', 'col')), may hold values from -5 to 6
- teacher: bfloat16 [12288, 512], P(('pb', 'col')), may hold values from -60 to 410
- tile_mask: int32 [96, 4], P(('pb', 'col')), may hold values from 0 to 1, as said below
- weights: float32 [12288], P(('pb', 'col')), may hold values from 0.25 to 4
Outputs:
- query_grad: float32 [12288, 1024], P(('pb', 'col'))
- group_grad: float32 [1024, 1024], P(('pb', 'col'))
The draws below stay inside these ranges and needn't reach their ends.
Inputs may be any that keep to these rules, and one draw needn't show every extreme that they name: `tile_mask`: every row of tiles has at least one 1; in every draw some rows of tiles are all ones.
All inputs are finite; a program needn't handle non-finite values.
Results may differ from the reference program's by a relative error of at most 0.0095.
Values may be sent and summed in bfloat16 or wider, within the bound.
No kernel may reach another device: no remote copies, remote signals or barrier semaphores. Data moves between devices by JAX's collectives and lax.ppermute only.
A program may use at most 64 MiB of HBM per device.

```python
import math
import jax
import jax.numpy as jnp
from jax import lax

D = 1024
QUERY_DEV = 384
STEPS = 4
TILE = 128
PANEL = 128
WINDOW = 512
QBLOCK = 1536
QUERIES = 12288
GROUPS = 1024
N_PB = 8
N_COL = 4


def draw_queries(key, part):
    key = jax.random.fold_in(key, 11)
    base_key = jax.random.fold_in(key, 0)
    values = jnp.clip(jax.random.normal(base_key, (QUERIES, D), jnp.float32), -5.0, 5.0)
    return values.astype(jnp.bfloat16)


def draw_groups(key, part):
    key = jax.random.fold_in(key, 23)
    values = jnp.clip(jax.random.normal(key, (GROUPS, D), jnp.float32), -5.0, 5.0)
    return values.astype(jnp.bfloat16)


def draw_teacher(key, part):
    key = jax.random.fold_in(key, 37)
    base_key, row_key, col_key = jax.random.split(key, 3)
    values = jnp.clip(jax.random.normal(base_key, (QUERIES, WINDOW), jnp.float32), -4.0, 4.0)
    row_scale = jnp.exp(jax.random.uniform(row_key, (QUERIES, 1), minval=math.log(0.3), maxval=math.log(3.0)))
    col_scale = jnp.exp(jax.random.uniform(col_key, (1, WINDOW), minval=math.log(0.5), maxval=math.log(5.0)))
    values = values * row_scale * col_scale
    return values.astype(jnp.bfloat16)


def draw_tile_mask(key, part):
    key = jax.random.fold_in(key, 53)
    count_key, perm_key = jax.random.split(key)
    tile_rows = QUERIES // TILE
    tile_cols = WINDOW // TILE
    counts = jax.random.randint(count_key, (tile_rows, 1), 1, tile_cols + 1)
    counts = jnp.where(jnp.arange(tile_rows)[:, None] % 5 == 0, tile_cols, counts)
    ranks = jax.vmap(lambda row_key: jax.random.permutation(row_key, tile_cols))(jax.random.split(perm_key, tile_rows))
    return (ranks < counts).astype(jnp.int32)


def level_of(key, shape, shards, smallest, largest):
    factor_of = 1.0
    for dim, blocks in shards:
        steps = jax.random.uniform(jax.random.fold_in(jax.random.fold_in(key, 6), dim), (blocks,), jnp.float32, smallest / len(shards), largest / len(shards))
        factor_of = factor_of * jnp.repeat(jnp.exp(steps), shape[dim] // blocks).reshape((-1,) + (1,) * (len(shape) - 1 - dim))
    return factor_of


def setup_inputs(seed: int = 0) -> dict:
    streams_of = jax.random.split(jax.random.key(seed), 6)
    queries = draw_queries(jax.random.fold_in(streams_of[5], 71), 0)
    groups = draw_groups(jax.random.fold_in(streams_of[5], 71), 0)
    teacher = draw_teacher(jax.random.fold_in(streams_of[5], 71), 0)
    tile_mask = draw_tile_mask(jax.random.fold_in(streams_of[5], 71), 0)
    weights = jnp.clip(jnp.exp(math.log(4.0) - 2.7725887 * jax.random.uniform(streams_of[4], (QUERIES,), jnp.float32) ** level_of(streams_of[4], (QUERIES,), ((0, 32),), -0.2, 0.2)), 0.25, 4.0)
    return {"queries": queries, "groups": groups, "teacher": teacher, "tile_mask": tile_mask, "weights": weights}


def masked_softmax(values, live_mask):
    row_max = lax.optimization_barrier(jnp.max(jnp.where(live_mask, values, -jnp.inf), axis=1, keepdims=True))
    expon = jnp.where(live_mask, jnp.exp(values - row_max), 0.0)
    return expon / lax.optimization_barrier(jnp.sum(expon, axis=1, keepdims=True))

def reference(queries, groups, teacher, tile_mask, weights):
    score_scale = 2.0 / math.sqrt(D)
    query_blocks = queries.reshape(N_PB, QBLOCK, D)
    teach_blocks = teacher.reshape(N_PB, QBLOCK, WINDOW)
    mask_blocks = tile_mask.reshape(N_PB, QBLOCK // TILE, WINDOW // TILE)
    weight_blocks = weights.reshape(N_PB, QBLOCK)
    panels = groups.reshape(N_PB, PANEL, D)

    def one_block(totals, inputs):
        block_index, query_rows, teach_rows, mask_rows, weight_rows = inputs
        panel_order = ((block_index - jnp.arange(STEPS, dtype=jnp.int32)) % N_PB).astype(jnp.int32)
        window_rows = panels[panel_order].reshape(WINDOW, D)
        scores = jnp.dot(query_rows, window_rows.T, preferred_element_type=jnp.float32) * score_scale
        live_mask = jnp.repeat(jnp.repeat(mask_rows, TILE, axis=0), TILE, axis=1) > 0
        student = masked_softmax(scores, live_mask)
        target = masked_softmax(teach_rows.astype(jnp.float32), live_mask)
        grads = ((weight_rows * score_scale)[:, None] * (student - target)).astype(jnp.bfloat16)
        query_part = jnp.dot(grads, window_rows, preferred_element_type=jnp.float32)
        per_device = jnp.einsum('jqw,jqd->jwd', grads.reshape(N_COL, QUERY_DEV, WINDOW).astype(jnp.float32), query_rows.reshape(N_COL, QUERY_DEV, D).astype(jnp.float32))
        rounded = lax.optimization_barrier(per_device.astype(jnp.bfloat16)).astype(jnp.float32)
        summed = lax.optimization_barrier(jnp.sum(rounded, axis=0)).reshape(STEPS, PANEL, D)
        totals = totals.at[panel_order].add(summed)
        return (totals, query_part)
    group_total, query_parts = lax.scan(one_block, jnp.zeros((N_PB, PANEL, D), jnp.float32), (jnp.arange(N_PB, dtype=jnp.int32), query_blocks, teach_blocks, mask_blocks, weight_blocks))
    return (query_parts.reshape(QUERIES, D), group_total.reshape(GROUPS, D))
```

```python
import functools
import math

import jax
import jax.numpy as jnp
from jax import lax
from jax.experimental import pallas as pl
from jax.experimental.pallas import tpu as pltpu
from jax.sharding import PartitionSpec as P

very_negative = -1e30


def passed_along(block, distance):
    count = lax.axis_size("pb")
    return lax.ppermute(block, "pb", [(i, (i + distance) % count) for i in range(count)])


def swapped(block, bit):
    return lax.ppermute(block, "col", [(i, i ^ bit) for i in range(lax.axis_size("col"))])


def live_scores(values, mask_ref, row_tile, tile_cols):
    parts = []
    for col_tile in range(mask_ref.shape[1]):
        part = values[:, col_tile * tile_cols : (col_tile + 1) * tile_cols]
        parts.append(jnp.where(mask_ref[row_tile, col_tile] > 0, part, very_negative))
    return jnp.concatenate(parts, axis=1)


def softmax_rows(values):
    expon = jnp.exp(values - jnp.max(values, axis=1, keepdims=True))
    return expon * (1.0 / jnp.sum(expon, axis=1, keepdims=True))


def target_kernel(mask_ref, teacher_ref, target_ref):
    tiles, tile_count = mask_ref.shape
    tile_rows = teacher_ref.shape[0] // tiles
    tile_cols = teacher_ref.shape[1] // tile_count
    for tile in range(tiles):
        rows = slice(tile * tile_rows, (tile + 1) * tile_rows)
        taught = teacher_ref[rows, :].astype(jnp.float32)
        target_ref[rows, :] = softmax_rows(live_scores(taught, mask_ref, tile, tile_cols))


def load_window(pieces, window_ref, sems, order, own_rows, own_col):
    copies = []
    for number, (step, offset) in enumerate(order):
        count_cols = len(order) // (1 + max(s for s, _ in order))
        row = (step * count_cols + (own_col ^ offset)) * own_rows
        copies.append(
            pltpu.make_async_copy(
                pieces[number],
                window_ref.at[pl.ds(pl.multiple_of(row, own_rows), own_rows), :],
                sems.at[number],
            )
        )
    for copy in copies:
        copy.start()
    return copies


def grads_kernel(order, score_scale, mask_ref, queries_ref, target_ref, weights_ref, *refs):
    pieces = refs[: len(order)]
    grads_ref, send_ref, keep_ref, window_ref, sems = refs[len(order) :]
    own_rows = pieces[0].shape[0]
    own_col = lax.axis_index("col")
    copies = load_window(pieces, window_ref, sems, order, own_rows, own_col)
    tiles, tile_count = mask_ref.shape
    tile_rows = queries_ref.shape[0] // tiles
    tile_cols = window_ref.shape[0] // tile_count
    for copy in copies:
        copy.wait()
    for tile in range(tiles):
        rows = slice(tile * tile_rows, (tile + 1) * tile_rows)
        scores = score_scale * lax.dot_general(
            queries_ref[rows, :],
            window_ref[...],
            (((1,), (1,)), ((), ())),
            preferred_element_type=jnp.float32,
        )
        student = softmax_rows(live_scores(scores, mask_ref, tile, tile_cols))
        grads = (weights_ref[rows, :] * score_scale) * (student - target_ref[rows, :])
        grads_ref[rows, :] = grads.astype(jnp.bfloat16)
    steps, halves = send_ref.shape[:2]
    panel = 2 * halves * own_rows
    for step in range(steps):
        term = lax.dot_general(
            grads_ref[:, step * panel : (step + 1) * panel],
            queries_ref[...],
            (((0,), (0,)), ((), ())),
            preferred_element_type=jnp.float32,
        ).astype(jnp.bfloat16)
        for col in range(2 * halves):
            part = term[col * own_rows : (col + 1) * own_rows, :]
            offset = own_col ^ col

            @pl.when(offset % 2 == 1)
            def _():
                send_ref[step, offset // 2] = part

            @pl.when(offset % 2 == 0)
            def _():
                keep_ref[step, offset // 2] = part


def query_grad_kernel(order, grads_ref, *refs):
    pieces = refs[: len(order)]
    out_ref, window_ref, sems = refs[len(order) :]
    own_rows = pieces[0].shape[0]
    copies = load_window(pieces, window_ref, sems, order, own_rows, lax.axis_index("col"))
    for copy in copies:
        copy.wait()
    out_ref[...] = jnp.dot(grads_ref[...], window_ref[...], preferred_element_type=jnp.float32)


def on_device(queries, groups, teacher, tile_mask, weights):
    count_rows, width = queries.shape
    score_scale = 2.0 / math.sqrt(width)
    own_rows = groups.shape[0]
    count_cols = lax.axis_size("col")
    window = teacher.shape[1]
    steps = window // (own_rows * count_cols)
    bits = [1 << k for k in reversed(range(count_cols.bit_length() - 1))]
    vmem = pl.BlockSpec(memory_space=pltpu.VMEM)
    smem = pl.BlockSpec(memory_space=pltpu.SMEM)
    far = pl.BlockSpec(memory_space=pl.ANY)
    budget = 16 * 2**20 + 2 * window * width * 2 + 2 * count_rows * (window + width) * 4

    target = pl.pallas_call(
        target_kernel,
        out_shape=jax.ShapeDtypeStruct((count_rows, window), jnp.float32),
        in_specs=[smem, vmem],
        out_specs=vmem,
        compiler_params=pltpu.CompilerParams(vmem_limit_bytes=budget),
        cost_estimate=pl.CostEstimate(
            flops=8 * count_rows * window,
            bytes_accessed=6 * count_rows * window,
            transcendentals=count_rows * window,
        ),
    )(tile_mask, teacher)

    held = {}
    for step in reversed(range(steps)):
        held[(step, 0)] = groups if step == 0 else passed_along(groups, step)
    for bit in bits:
        for step, offset in list(held):
            held[(step, offset ^ bit)] = swapped(held[(step, offset)], bit)
    order = sorted(held)
    pieces = [held[key] for key in order]

    grads, send, keep = pl.pallas_call(
        functools.partial(grads_kernel, order, score_scale),
        out_shape=(
            jax.ShapeDtypeStruct((count_rows, window), jnp.bfloat16),
            jax.ShapeDtypeStruct((steps, count_cols // 2, own_rows, width), jnp.bfloat16),
            jax.ShapeDtypeStruct((steps, count_cols // 2, own_rows, width), jnp.bfloat16),
        ),
        in_specs=[smem, vmem, vmem, vmem] + [far] * len(pieces),
        out_specs=(vmem, vmem, vmem),
        scratch_shapes=[
            pltpu.VMEM((window, width), jnp.bfloat16),
            pltpu.SemaphoreType.DMA((len(pieces),)),
        ],
        compiler_params=pltpu.CompilerParams(vmem_limit_bytes=budget),
        cost_estimate=pl.CostEstimate(
            flops=4 * count_rows * window * width,
            bytes_accessed=2 * count_rows * width + 4 * window * width + 6 * count_rows * window,
            transcendentals=count_rows * window,
        ),
    )(tile_mask, queries, target, weights[:, None], *pieces)

    query_grad = pl.pallas_call(
        functools.partial(query_grad_kernel, order),
        out_shape=jax.ShapeDtypeStruct((count_rows, width), jnp.float32),
        in_specs=[vmem] + [far] * len(pieces),
        out_specs=vmem,
        scratch_shapes=[
            pltpu.VMEM((window, width), jnp.bfloat16),
            pltpu.SemaphoreType.DMA((len(pieces),)),
        ],
        compiler_params=pltpu.CompilerParams(vmem_limit_bytes=budget),
        cost_estimate=pl.CostEstimate(
            flops=2 * count_rows * window * width,
            bytes_accessed=4 * count_rows * width + 2 * window * width + 2 * count_rows * window,
            transcendentals=0,
        ),
    )(grads, *pieces)

    group_grad = None
    for step in reversed(range(steps)):
        total = keep[step].astype(jnp.float32) + swapped(send[step], 1).astype(jnp.float32)
        for bit in reversed(bits[:-1]):
            half = total.reshape(-1, 2, own_rows, width)
            total = half[:, 0].astype(jnp.float32) + swapped(
                half[:, 1].astype(jnp.bfloat16), bit
            ).astype(jnp.float32)
        total = total.reshape(own_rows, width)
        if step > 0:
            total = passed_along(total.astype(jnp.bfloat16), -step).astype(jnp.float32)
        group_grad = total if group_grad is None else group_grad + total
    return (query_grad, group_grad)


def solution(mesh):
    placed = (
        P(("pb", "col"), None),
        P(("pb", "col"), None),
        P(("pb", "col"), None),
        P(("pb", "col"), None),
        P(("pb", "col")),
    )
    return jax.shard_map(
        on_device,
        mesh=mesh,
        in_specs=placed,
        out_specs=(P(("pb", "col"), None), P(("pb", "col"), None)),
        check_vma=False,
    )
```

```python
import functools
import math

import jax
import jax.numpy as jnp
from jax import lax
from jax.experimental import pallas as pl
from jax.experimental.pallas import tpu as pltpu
from jax.sharding import PartitionSpec as P

very_negative = -1e30


def moved_to(block, target):
    count_cols = lax.axis_size("col")
    pairs = []
    for p in range(lax.axis_size("pb")):
        for c in range(count_cols):
            q, d = target(p, c)
            pairs.append((p * count_cols + c, q * count_cols + d))
    return lax.ppermute(block, ("pb", "col"), pairs)


def swapped(block, bits):
    return moved_to(block, lambda p, c: (p, c ^ bits))


def softmax_cols(blocks):
    top = functools.reduce(jnp.maximum, [jnp.max(block, axis=0, keepdims=True) for block in blocks])
    blocks = [jnp.exp(block - top) for block in blocks]
    total = functools.reduce(jnp.add, [jnp.sum(block, axis=0, keepdims=True) for block in blocks])
    scale = 1.0 / total
    return [block * scale for block in blocks]


def piece_col(number, slot_steps, count_cols, own_rows):
    slot, offset = divmod(number, count_cols)
    own_step = slot_steps(lax.axis_index("pb"))[slot]
    own_col = lax.axis_index("col")
    return pl.multiple_of((own_step * count_cols + (own_col ^ offset)) * own_rows, own_rows)


def target_kernel(
    slot_steps, count_cols, score_scale, own_rows, mask_ref, weights_ref, teacher_ref, queries_ref,
    target_ref, live_ref, factor_ref, flat_ref,
):
    del queries_ref
    window, count_rows = target_ref.shape
    tiles, tile_count = mask_ref.shape
    tile_rows, tile_cols = count_rows // tiles, window // tile_count
    factor_ref[...] = weights_ref[...] * score_scale
    for tile in range(tiles):
        rows = slice(tile * tile_rows, (tile + 1) * tile_rows)
        taught = teacher_ref[rows, :].astype(jnp.float32).T
        blocks = []
        for col in range(tile_count):
            part = taught[col * tile_cols : (col + 1) * tile_cols, :]
            blocks.append(jnp.where(mask_ref[tile, col] > 0, part, very_negative))
        for col, block in enumerate(softmax_cols(blocks)):
            flat_ref[col * tile_cols : (col + 1) * tile_cols, rows] = block
    for number in range(window // own_rows):
        col = piece_col(number, slot_steps, count_cols, own_rows)
        target_ref[number * own_rows : (number + 1) * own_rows, :] = flat_ref[pl.ds(col, own_rows), :]
        for tile in range(tiles):
            live = mask_ref[tile, col // tile_cols].astype(jnp.float32)
            live_ref[number : number + 1, tile * tile_rows : (tile + 1) * tile_rows] = jnp.full(
                (1, tile_rows), live, jnp.float32
            )


def grads_kernel(score_scale, queries_ref, target_ref, live_ref, factor_ref, *refs):
    grads_ref, window_ref, send_ref, keep_ref, scores_ref = refs[-5:]
    pieces = refs[:-5]
    halves, own_rows = pieces[0].shape[:2]
    count_rows = grads_ref.shape[1]
    lanes = 128 if count_rows % 128 == 0 else count_rows
    for number in range(len(pieces) * halves):
        slot, offset = divmod(number, 2 * halves)
        window_ref[number * own_rows : (number + 1) * own_rows, :] = pieces[2 * slot + offset % 2][offset // 2]
    scores_ref[...] = score_scale * lax.dot_general(
        window_ref[...],
        queries_ref[...],
        (((1,), (1,)), ((), ())),
        preferred_element_type=jnp.float32,
    )
    for first in range(0, count_rows, lanes):
        rows = slice(first, first + lanes)
        blocks = []
        for number in range(len(pieces) * halves):
            part = scores_ref[number * own_rows : (number + 1) * own_rows, rows]
            blocks.append(jnp.where(live_ref[number : number + 1, rows] > 0, part, very_negative))
        factor = factor_ref[:, rows]
        for number, student in enumerate(softmax_cols(blocks)):
            cols = slice(number * own_rows, (number + 1) * own_rows)
            grads_ref[cols, rows] = (factor * (student - target_ref[cols, rows])).astype(jnp.bfloat16)
    slots = send_ref.shape[0]
    panel = 2 * halves * own_rows
    for slot in reversed(range(slots)):
        term = jnp.dot(
            grads_ref[slot * panel : (slot + 1) * panel, :],
            queries_ref[...],
            preferred_element_type=jnp.float32,
        ).astype(jnp.bfloat16)
        for half in range(halves):
            keep_ref[slot, half] = term[2 * half * own_rows : (2 * half + 1) * own_rows, :]
            send_ref[slot, half] = term[(2 * half + 1) * own_rows : (2 * half + 2) * own_rows, :]


def query_grad_kernel(grads_ref, window_ref, out_ref, part_ref, sems):
    count_rows = out_ref.shape[0]
    rows = part_ref.shape[1]
    copies = []
    for tile in range(count_rows // rows):
        part_ref[tile] = lax.dot_general(
            grads_ref[:, tile * rows : (tile + 1) * rows],
            window_ref[...],
            (((0,), (0,)), ((), ())),
            preferred_element_type=jnp.float32,
        )
        copy = pltpu.make_async_copy(
            part_ref.at[tile], out_ref.at[tile * rows : (tile + 1) * rows, :], sems.at[tile]
        )
        copy.start()
        copies.append(copy)
    for copy in copies:
        copy.wait()


def on_device(queries, groups, teacher, tile_mask, weights):
    count_rows, width = queries.shape
    score_scale = 2.0 / math.sqrt(width)
    own_rows = groups.shape[0]
    count_pb, count_cols = lax.axis_size("pb"), lax.axis_size("col")
    window = teacher.shape[1]
    steps = window // (own_rows * count_cols)
    tiles = tile_mask.shape[0]
    evens = range(0, count_cols, 2)
    vmem = pl.BlockSpec(memory_space=pltpu.VMEM)
    smem = pl.BlockSpec(memory_space=pltpu.SMEM)
    far = pl.BlockSpec(memory_space=pltpu.HBM)
    budget = 8 * 2**20 + 6 * window * width * 2 + 2 * count_rows * (window + width) * 4
    params = pltpu.CompilerParams(vmem_limit_bytes=min(budget, 50 * 2**20))

    def slot_steps(p):
        return (0, 2, 3 - 2 * (p % 2), 1 + 2 * (p % 2))

    def own(offset):
        return lambda p, c: (p, c ^ offset)

    def ahead(offset):
        return lambda p, c: ((p + 2) % count_pb, c ^ offset)

    def across(offset):
        return lambda p, c: ((p + 1 + 2 * (p % 2)) % count_pb, c ^ offset)

    def beside(p, c):
        return (p ^ 1, c)

    def reverse(move):
        back = {move(p, c): (p, c) for p in range(count_pb) for c in range(count_cols)}
        return lambda p, c: back[(p, c)]

    def joined(parts):
        return jnp.stack(parts)

    second = joined([moved_to(groups, ahead(offset)) for offset in evens])
    thirds = [moved_to(groups, across(offset)) for offset in evens]
    firsts = [groups] + [moved_to(groups, own(offset)) for offset in evens[1:]]
    fourth = moved_to(second, beside)

    teacher, queries, _ = lax.optimization_barrier((teacher, queries, second))
    target, live, factor = pl.pallas_call(
        functools.partial(target_kernel, slot_steps, count_cols, score_scale, own_rows),
        out_shape=(
            jax.ShapeDtypeStruct((window, count_rows), jnp.float32),
            jax.ShapeDtypeStruct((window // own_rows, count_rows), jnp.float32),
            jax.ShapeDtypeStruct((1, count_rows), jnp.float32),
        ),
        in_specs=[smem, vmem, vmem, vmem],
        out_specs=(vmem,) * 3,
        scratch_shapes=[pltpu.VMEM((window, count_rows), jnp.float32)],
        compiler_params=params,
        cost_estimate=pl.CostEstimate(
            flops=8 * count_rows * window,
            bytes_accessed=6 * count_rows * (window + width),
            transcendentals=count_rows * window,
        ),
    )(tile_mask, weights[None, :], teacher, queries)
    thirds, target = lax.optimization_barrier((thirds, target))
    firsts, target = lax.optimization_barrier((firsts, target))
    fourth, target = lax.optimization_barrier((fourth, target))
    first, third = joined(firsts), joined(thirds)
    held = [first, second, third, fourth]
    pieces = []
    for block in held:
        pieces += [block, moved_to(block, own(1))]

    grads, gathered, send, keep = pl.pallas_call(
        functools.partial(grads_kernel, score_scale),
        out_shape=(
            jax.ShapeDtypeStruct((window, count_rows), jnp.bfloat16),
            jax.ShapeDtypeStruct((window, width), jnp.bfloat16),
            jax.ShapeDtypeStruct((steps, count_cols // 2, own_rows, width), jnp.bfloat16),
            jax.ShapeDtypeStruct((steps, count_cols // 2, own_rows, width), jnp.bfloat16),
        ),
        in_specs=[vmem] * (4 + len(pieces)),
        out_specs=(vmem,) * 4,
        scratch_shapes=[pltpu.VMEM((window, count_rows), jnp.float32)],
        compiler_params=params,
        cost_estimate=pl.CostEstimate(
            flops=4 * count_rows * window * width,
            bytes_accessed=2 * count_rows * width + 4 * window * width + 6 * count_rows * window,
            transcendentals=count_rows * window,
        ),
    )(queries, target, live, factor, *pieces)

    rows = count_rows // tiles
    query_grad = pl.pallas_call(
        query_grad_kernel,
        out_shape=jax.ShapeDtypeStruct((count_rows, width), jnp.float32),
        in_specs=[vmem, vmem],
        out_specs=far,
        scratch_shapes=[
            pltpu.VMEM((tiles, rows, width), jnp.float32),
            pltpu.SemaphoreType.DMA((tiles,)),
        ],
        compiler_params=params,
        cost_estimate=pl.CostEstimate(
            flops=2 * count_rows * window * width,
            bytes_accessed=4 * count_rows * width + 2 * window * width + 2 * count_rows * window,
            transcendentals=0,
        ),
    )(grads, gathered)

    sums = []
    for slot in range(steps):
        other = swapped(send[slot], 1)
        sums.append(keep[slot].astype(jnp.float32) + other.astype(jnp.float32))

    def arrived(block, move):
        return moved_to(block.astype(jnp.bfloat16), move).astype(jnp.float32)

    sums[1] = sums[1] + arrived(sums[3], beside)
    moves = ((2, across), (1, ahead), (0, own))
    group_grad = sums[0][0]
    for slot, move in moves:
        for offset in evens:
            if slot > 0 or offset > 0:
                group_grad = group_grad + arrived(sums[slot][offset // 2], reverse(move(offset)))
    return (query_grad, group_grad)


def solution(mesh):
    placed = (
        P(("pb", "col"), None),
        P(("pb", "col"), None),
        P(("pb", "col"), None),
        P(("pb", "col"), None),
        P(("pb", "col")),
    )
    return jax.shard_map(
        on_device,
        mesh=mesh,
        in_specs=placed,
        out_specs=(P(("pb", "col"), None), P(("pb", "col"), None)),
        check_vma=False,
    )
```

```python
import functools
import math

import jax
import jax.numpy as jnp
from jax import lax
from jax.experimental import pallas as pl
from jax.experimental.pallas import tpu as pltpu
from jax.sharding import PartitionSpec as P

very_negative = -1e30


def moved_to(block, target):
    count_cols = lax.axis_size("col")
    pairs = []
    for p in range(lax.axis_size("pb")):
        for c in range(count_cols):
            q, d = target(p, c)
            pairs.append((p * count_cols + c, q * count_cols + d))
    return lax.ppermute(block, ("pb", "col"), pairs)


def swapped(block, bits):
    return moved_to(block, lambda p, c: (p, c ^ bits))


def softmax_cols(blocks):
    top = functools.reduce(jnp.maximum, [jnp.max(block, axis=0, keepdims=True) for block in blocks])
    blocks = [jnp.exp(block - top) for block in blocks]
    total = functools.reduce(jnp.add, [jnp.sum(block, axis=0, keepdims=True) for block in blocks])
    scale = 1.0 / total
    return [block * scale for block in blocks]


def piece_col(number, slot_steps, count_cols, own_rows):
    slot, offset = divmod(number, count_cols)
    own_step = slot_steps(lax.axis_index("pb"))[slot]
    own_col = lax.axis_index("col")
    return pl.multiple_of((own_step * count_cols + (own_col ^ offset)) * own_rows, own_rows)


def target_kernel(slot_steps, count_cols, own_rows, mask_ref, packed_ref, target_ref, flat_ref):
    window, count_rows = target_ref.shape
    width = packed_ref.shape[1] - window
    tiles, tile_count = mask_ref.shape
    tile_rows, tile_cols = count_rows // tiles, window // tile_count
    for tile in range(tiles):
        rows = slice(tile * tile_rows, (tile + 1) * tile_rows)
        taught = packed_ref[rows, width:].astype(jnp.float32).T
        lives, blocks = [], []
        for col in range(tile_count):
            part = taught[col * tile_cols : (col + 1) * tile_cols, :]
            live = jnp.broadcast_to(mask_ref[tile : tile + 1, col : col + 1], part.shape) > 0
            lives.append(live)
            blocks.append(jnp.where(live, part, very_negative))
        for col, block in enumerate(softmax_cols(blocks)):
            flat_ref[col * tile_cols : (col + 1) * tile_cols, :] = jnp.where(lives[col], block, -1.0)
        for number in range(window // own_rows):
            col = piece_col(number, slot_steps, count_cols, own_rows)
            target_ref[number * own_rows : (number + 1) * own_rows, rows] = flat_ref[pl.ds(col, own_rows), :]


def grads_kernel(score_scale, packed_ref, target_ref, weights_ref, *refs):
    grads_ref, window_ref, send_ref, keep_ref, scores_ref = refs[-5:]
    pieces = refs[:-5]
    halves, own_rows, width = pieces[0].shape
    count_rows = grads_ref.shape[1]
    lanes = 128 if count_rows % 128 == 0 else count_rows
    for number in range(len(pieces) * halves):
        slot, offset = divmod(number, 2 * halves)
        window_ref[number * own_rows : (number + 1) * own_rows, :] = pieces[2 * slot + offset % 2][offset // 2]
    scores_ref[...] = score_scale * lax.dot_general(
        window_ref[...],
        packed_ref[:count_rows, :width],
        (((1,), (1,)), ((), ())),
        preferred_element_type=jnp.float32,
    )
    for first in range(0, count_rows, lanes):
        rows = slice(first, first + lanes)
        target = target_ref[:, rows]
        (student,) = softmax_cols([jnp.where(target >= 0, scores_ref[:, rows], very_negative)])
        factor = weights_ref[:, rows] * score_scale
        grads_ref[:, rows] = (factor * (student - jnp.maximum(target, 0.0))).astype(jnp.bfloat16)
    slots = send_ref.shape[0]
    panel = 2 * halves * own_rows
    for slot in reversed(range(slots)):
        term = jnp.dot(
            grads_ref[slot * panel : (slot + 1) * panel, :],
            packed_ref[:count_rows, :width],
            preferred_element_type=jnp.float32,
        ).astype(jnp.bfloat16)
        for half in range(halves):
            keep_ref[slot, half] = term[2 * half * own_rows : (2 * half + 1) * own_rows, :]
            send_ref[slot, half] = term[(2 * half + 1) * own_rows : (2 * half + 2) * own_rows, :]


def query_grad_kernel(grads_ref, window_ref, out_ref, part_ref, sems):
    count_rows = out_ref.shape[0]
    rows = part_ref.shape[1]
    copies = []
    for tile in range(count_rows // rows):
        part_ref[tile] = lax.dot_general(
            grads_ref[:, tile * rows : (tile + 1) * rows],
            window_ref[...],
            (((0,), (0,)), ((), ())),
            preferred_element_type=jnp.float32,
        )
        copy = pltpu.make_async_copy(
            part_ref.at[tile], out_ref.at[tile * rows : (tile + 1) * rows, :], sems.at[tile]
        )
        copy.start()
        copies.append(copy)
    for copy in copies:
        copy.wait()


def on_device(queries, groups, teacher, tile_mask, weights):
    count_rows, width = queries.shape
    score_scale = 2.0 / math.sqrt(width)
    own_rows = groups.shape[0]
    count_pb, count_cols = lax.axis_size("pb"), lax.axis_size("col")
    window = teacher.shape[1]
    steps = window // (own_rows * count_cols)
    tiles = tile_mask.shape[0]
    evens = range(0, count_cols, 2)
    vmem = pl.BlockSpec(memory_space=pltpu.VMEM)
    far = pl.BlockSpec(memory_space=pltpu.HBM)
    budget = 8 * 2**20 + 6 * window * width * 2 + 2 * count_rows * (window + width) * 4
    params = pltpu.CompilerParams(vmem_limit_bytes=min(budget, 50 * 2**20))

    def slot_steps(p):
        return (0, 2, 3 - 2 * (p % 2), 1 + 2 * (p % 2))

    def own(offset):
        return lambda p, c: (p, c ^ offset)

    def ahead(offset):
        return lambda p, c: ((p + 2) % count_pb, c ^ offset)

    def across(offset):
        return lambda p, c: ((p + 1 + 2 * (p % 2)) % count_pb, c ^ offset)

    def beside(p, c):
        return (p ^ 1, c)

    def reverse(move):
        back = {move(p, c): (p, c) for p in range(count_pb) for c in range(count_cols)}
        return lambda p, c: back[(p, c)]

    def after(value, *others):
        return lax.optimization_barrier((value, *others))[0]

    seconds = [moved_to(groups, ahead(offset)) for offset in evens]
    third = moved_to(groups, across(0))
    packed = jnp.concatenate(
        [
            jnp.concatenate([queries, teacher], axis=1),
            jnp.pad(groups, ((0, 0), (0, window))),
        ],
        axis=0,
    )
    seconds = [after(seconds[0], packed)] + seconds[1:]
    fourths = [moved_to(block, beside) for block in seconds]
    late_packed = after(packed, fourths[0])
    target = pl.pallas_call(
        functools.partial(target_kernel, slot_steps, count_cols, own_rows),
        out_shape=jax.ShapeDtypeStruct((window, count_rows), jnp.float32),
        in_specs=[vmem, vmem],
        out_specs=vmem,
        scratch_shapes=[pltpu.VMEM((window, count_rows // tiles), jnp.float32)],
        compiler_params=params,
        cost_estimate=pl.CostEstimate(
            flops=8 * count_rows * window,
            bytes_accessed=6 * count_rows * window,
            transcendentals=count_rows * window,
        ),
    )(tile_mask, late_packed)
    near_groups = after(groups, seconds[0])
    firsts = [near_groups] + [moved_to(near_groups, own(offset)) for offset in evens[1:]]
    thirds = [third] + [moved_to(third, own(offset)) for offset in evens[1:]]
    pieces = []
    for blocks in (firsts, seconds, thirds, fourths):
        block = jnp.stack(blocks)
        pieces += [block, moved_to(block, own(1))]

    grads, gathered, send, keep = pl.pallas_call(
        functools.partial(grads_kernel, score_scale),
        out_shape=(
            jax.ShapeDtypeStruct((window, count_rows), jnp.bfloat16),
            jax.ShapeDtypeStruct((window, width), jnp.bfloat16),
            jax.ShapeDtypeStruct((steps, count_cols // 2, own_rows, width), jnp.bfloat16),
            jax.ShapeDtypeStruct((steps, count_cols // 2, own_rows, width), jnp.bfloat16),
        ),
        in_specs=[vmem] * (3 + len(pieces)),
        out_specs=(vmem,) * 4,
        scratch_shapes=[pltpu.VMEM((window, count_rows), jnp.float32)],
        compiler_params=params,
        cost_estimate=pl.CostEstimate(
            flops=4 * count_rows * window * width,
            bytes_accessed=2 * count_rows * width + 4 * window * width + 6 * count_rows * window,
            transcendentals=count_rows * window,
        ),
    )(packed, target, weights[None, :], *pieces)

    rows = count_rows // tiles
    query_grad = pl.pallas_call(
        query_grad_kernel,
        out_shape=jax.ShapeDtypeStruct((count_rows, width), jnp.float32),
        in_specs=[vmem, vmem],
        out_specs=far,
        scratch_shapes=[
            pltpu.VMEM((tiles, rows, width), jnp.float32),
            pltpu.SemaphoreType.DMA((tiles,)),
        ],
        compiler_params=params,
        cost_estimate=pl.CostEstimate(
            flops=2 * count_rows * window * width,
            bytes_accessed=4 * count_rows * width + 2 * window * width + 2 * count_rows * window,
            transcendentals=0,
        ),
    )(grads, gathered)

    def arrived(block, move):
        return moved_to(block.astype(jnp.bfloat16), move).astype(jnp.float32)

    sums = {}
    last = None
    for slot in (3, 2, 1, 0):
        other = moved_to(send[slot], own(1))
        if last is not None:
            other = after(other, last)
        last = keep[slot].astype(jnp.float32) + other.astype(jnp.float32)
        sums[slot] = [last[offset // 2] for offset in evens]
    third = sums[2][0]
    for offset in evens[1:]:
        third = third + arrived(sums[2][offset // 2], own(offset))
    seconds = [part + arrived(fourth, beside) for part, fourth in zip(sums[1], sums[3])]
    group_grad = sums[0][0] + arrived(third, reverse(across(0)))
    for offset in evens:
        group_grad = group_grad + arrived(seconds[offset // 2], reverse(ahead(offset)))
    for offset in evens[1:]:
        group_grad = group_grad + arrived(sums[0][offset // 2], own(offset))
    return (query_grad, group_grad)


def solution(mesh):
    placed = (
        P(("pb", "col"), None),
        P(("pb", "col"), None),
        P(("pb", "col"), None),
        P(("pb", "col"), None),
        P(("pb", "col")),
    )
    return jax.shard_map(
        on_device,
        mesh=mesh,
        in_specs=placed,
        out_specs=(P(("pb", "col"), None), P(("pb", "col"), None)),
        check_vma=False,
    )
```

```python
import functools
import math

import jax
import jax.numpy as jnp
from jax import lax
from jax.experimental import pallas as pl
from jax.experimental.pallas import tpu as pltpu
from jax.sharding import PartitionSpec as P

very_negative = -1e30


def moved_to(block, target):
    count_cols = lax.axis_size("col")
    pairs = []
    for p in range(lax.axis_size("pb")):
        for c in range(count_cols):
            q, d = target(p, c)
            pairs.append((p * count_cols + c, q * count_cols + d))
    return lax.ppermute(block, ("pb", "col"), pairs)


def swapped(block, bits):
    return moved_to(block, lambda p, c: (p, c ^ bits))


def softmax_cols(blocks):
    top = functools.reduce(jnp.maximum, [jnp.max(block, axis=0, keepdims=True) for block in blocks])
    blocks = [jnp.exp(block - top) for block in blocks]
    total = functools.reduce(jnp.add, [jnp.sum(block, axis=0, keepdims=True) for block in blocks])
    scale = 1.0 / total
    return [block * scale for block in blocks]


def piece_col(number, slot_steps, count_cols, own_rows):
    slot, offset = divmod(number, count_cols)
    own_step = slot_steps(lax.axis_index("pb"))[slot]
    own_col = lax.axis_index("col")
    return pl.multiple_of((own_step * count_cols + (own_col ^ offset)) * own_rows, own_rows)


def target_kernel(slot_steps, count_cols, own_rows, mask_ref, packed_ref, target_ref, flat_ref):
    window, count_rows = target_ref.shape
    width = packed_ref.shape[1] - window
    tiles, tile_count = mask_ref.shape
    tile_rows, tile_cols = count_rows // tiles, window // tile_count
    for tile in range(tiles):
        rows = slice(tile * tile_rows, (tile + 1) * tile_rows)
        taught = packed_ref[rows, width:].astype(jnp.float32).T
        lives, blocks = [], []
        for col in range(tile_count):
            part = taught[col * tile_cols : (col + 1) * tile_cols, :]
            live = jnp.broadcast_to(mask_ref[tile : tile + 1, col : col + 1], part.shape) > 0
            lives.append(live)
            blocks.append(jnp.where(live, part, very_negative))
        for col, block in enumerate(softmax_cols(blocks)):
            flat_ref[col * tile_cols : (col + 1) * tile_cols, :] = jnp.where(lives[col], block, -1.0)
        for number in range(window // own_rows):
            col = piece_col(number, slot_steps, count_cols, own_rows)
            target_ref[number * own_rows : (number + 1) * own_rows, rows] = flat_ref[pl.ds(col, own_rows), :]


def grads_kernel(score_scale, places, packed_ref, target_ref, weights_ref, *refs):
    grads_ref, window_ref, send_ref, keep_ref, scores_ref = refs[-5:]
    pieces = refs[:-5]
    own_rows, width = pieces[0].shape[1:]
    count_rows = grads_ref.shape[1]
    lanes = 128 if count_rows % 128 == 0 else count_rows
    slots, halves = send_ref.shape[:2]
    for number in range(slots * 2 * halves):
        slot, offset = divmod(number, 2 * halves)
        index, place = places[slot]
        window_ref[number * own_rows : (number + 1) * own_rows, :] = pieces[index + offset % 2][place + offset // 2]
    scores_ref[...] = score_scale * lax.dot_general(
        window_ref[...],
        packed_ref[:count_rows, :width],
        (((1,), (1,)), ((), ())),
        preferred_element_type=jnp.float32,
    )
    for first in range(0, count_rows, lanes):
        rows = slice(first, first + lanes)
        target = target_ref[:, rows]
        (student,) = softmax_cols([jnp.where(target >= 0, scores_ref[:, rows], very_negative)])
        factor = weights_ref[:, rows] * score_scale
        grads_ref[:, rows] = (factor * (student - jnp.maximum(target, 0.0))).astype(jnp.bfloat16)
    panel = 2 * halves * own_rows
    for slot in reversed(range(slots)):
        term = jnp.dot(
            grads_ref[slot * panel : (slot + 1) * panel, :],
            packed_ref[:count_rows, :width],
            preferred_element_type=jnp.float32,
        ).astype(jnp.bfloat16)
        for half in range(halves):
            keep_ref[slot, half] = term[2 * half * own_rows : (2 * half + 1) * own_rows, :]
            send_ref[slot, half] = term[(2 * half + 1) * own_rows : (2 * half + 2) * own_rows, :]


def query_grad_kernel(grads_ref, window_ref, out_ref, part_ref, sems):
    count_rows = out_ref.shape[0]
    rows = part_ref.shape[1]
    copies = []
    for tile in range(count_rows // rows):
        part_ref[tile] = lax.dot_general(
            grads_ref[:, tile * rows : (tile + 1) * rows],
            window_ref[...],
            (((0,), (0,)), ((), ())),
            preferred_element_type=jnp.float32,
        )
        copy = pltpu.make_async_copy(
            part_ref.at[tile], out_ref.at[tile * rows : (tile + 1) * rows, :], sems.at[tile]
        )
        copy.start()
        copies.append(copy)
    for copy in copies:
        copy.wait()


def on_device(queries, groups, teacher, tile_mask, weights):
    count_rows, width = queries.shape
    score_scale = 2.0 / math.sqrt(width)
    own_rows = groups.shape[0]
    count_pb, count_cols = lax.axis_size("pb"), lax.axis_size("col")
    window = teacher.shape[1]
    steps = window // (own_rows * count_cols)
    tiles = tile_mask.shape[0]
    evens = range(0, count_cols, 2)
    vmem = pl.BlockSpec(memory_space=pltpu.VMEM)
    far = pl.BlockSpec(memory_space=pltpu.HBM)
    budget = 8 * 2**20 + 6 * window * width * 2 + 2 * count_rows * (window + width) * 4
    params = pltpu.CompilerParams(vmem_limit_bytes=min(budget, 50 * 2**20))

    def slot_steps(p):
        return (0, 2, 3 - 2 * (p % 2), 1 + 2 * (p % 2))

    def own(offset):
        return lambda p, c: (p, c ^ offset)

    def ahead(offset):
        return lambda p, c: ((p + 2) % count_pb, c ^ offset)

    def across(offset):
        return lambda p, c: ((p + 1 + 2 * (p % 2)) % count_pb, c ^ offset)

    def beside(p, c):
        return (p ^ 1, c)

    def reverse(move):
        back = {move(p, c): (p, c) for p in range(count_pb) for c in range(count_cols)}
        return lambda p, c: back[(p, c)]

    def after(value, *others):
        return lax.optimization_barrier((value, *others))[0]

    seconds = [moved_to(groups, ahead(offset)) for offset in evens]
    third = moved_to(groups, across(0))
    packed = jnp.concatenate(
        [
            jnp.concatenate([queries, teacher], axis=1),
            jnp.pad(groups, ((0, 0), (0, window))),
        ],
        axis=0,
    )
    seconds = [after(seconds[0], packed)] + seconds[1:]
    fourths = [moved_to(block, beside) for block in seconds]
    late_packed = after(packed, fourths[0])
    target = pl.pallas_call(
        functools.partial(target_kernel, slot_steps, count_cols, own_rows),
        out_shape=jax.ShapeDtypeStruct((window, count_rows), jnp.float32),
        in_specs=[vmem, vmem],
        out_specs=vmem,
        scratch_shapes=[pltpu.VMEM((window, count_rows // tiles), jnp.float32)],
        compiler_params=params,
        cost_estimate=pl.CostEstimate(
            flops=8 * count_rows * window,
            bytes_accessed=6 * count_rows * window,
            transcendentals=count_rows * window,
        ),
    )(tile_mask, late_packed)
    near_groups = after(groups, seconds[0])
    firsts = [near_groups] + [moved_to(near_groups, own(offset)) for offset in evens[1:]]
    thirds = [third] + [moved_to(third, own(offset)) for offset in evens[1:]]
    blocks = (firsts, seconds, thirds, fourths)
    pieces, places = [], {}
    for together in ((0, 1), (2, 3)):
        block = jnp.stack([part for slot in together for part in blocks[slot]])
        for place, slot in enumerate(together):
            places[slot] = (len(pieces), place * len(evens))
        pieces += [block, moved_to(block, own(1))]

    grads, gathered, send, keep = pl.pallas_call(
        functools.partial(grads_kernel, score_scale, places),
        out_shape=(
            jax.ShapeDtypeStruct((window, count_rows), jnp.bfloat16),
            jax.ShapeDtypeStruct((window, width), jnp.bfloat16),
            jax.ShapeDtypeStruct((steps, count_cols // 2, own_rows, width), jnp.bfloat16),
            jax.ShapeDtypeStruct((steps, count_cols // 2, own_rows, width), jnp.bfloat16),
        ),
        in_specs=[vmem] * (3 + len(pieces)),
        out_specs=(vmem,) * 4,
        scratch_shapes=[pltpu.VMEM((window, count_rows), jnp.float32)],
        compiler_params=params,
        cost_estimate=pl.CostEstimate(
            flops=4 * count_rows * window * width,
            bytes_accessed=2 * count_rows * width + 4 * window * width + 6 * count_rows * window,
            transcendentals=count_rows * window,
        ),
    )(packed, target, weights[None, :], *pieces)

    rows = count_rows // tiles
    query_grad = pl.pallas_call(
        query_grad_kernel,
        out_shape=jax.ShapeDtypeStruct((count_rows, width), jnp.float32),
        in_specs=[vmem, vmem],
        out_specs=far,
        scratch_shapes=[
            pltpu.VMEM((tiles, rows, width), jnp.float32),
            pltpu.SemaphoreType.DMA((tiles,)),
        ],
        compiler_params=params,
        cost_estimate=pl.CostEstimate(
            flops=2 * count_rows * window * width,
            bytes_accessed=4 * count_rows * width + 2 * window * width + 2 * count_rows * window,
            transcendentals=0,
        ),
    )(grads, gathered)

    def arrived(block, move):
        return moved_to(block.astype(jnp.bfloat16), move).astype(jnp.float32)

    sums = {}
    last = None
    for slot in (3, 2, 1, 0):
        other = moved_to(send[slot], own(1))
        if last is not None:
            other = after(other, last)
        last = keep[slot].astype(jnp.float32) + other.astype(jnp.float32)
        sums[slot] = [last[offset // 2] for offset in evens]
    third = sums[2][0]
    for offset in evens[1:]:
        third = third + arrived(sums[2][offset // 2], own(offset))
    seconds = [part + arrived(fourth, beside) for part, fourth in zip(sums[1], sums[3])]
    group_grad = sums[0][0] + arrived(third, reverse(across(0)))
    for offset in evens:
        group_grad = group_grad + arrived(seconds[offset // 2], reverse(ahead(offset)))
    for offset in evens[1:]:
        group_grad = group_grad + arrived(sums[0][offset // 2], own(offset))
    return (query_grad, group_grad)


def solution(mesh):
    placed = (
        P(("pb", "col"), None),
        P(("pb", "col"), None),
        P(("pb", "col"), None),
        P(("pb", "col"), None),
        P(("pb", "col")),
    )
    return jax.shard_map(
        on_device,
        mesh=mesh,
        in_specs=placed,
        out_specs=(P(("pb", "col"), None), P(("pb", "col"), None)),
        check_vma=False,
    )
```

```python
import functools
import math

import jax
import jax.numpy as jnp
from jax import lax
from jax.experimental import pallas as pl
from jax.experimental.pallas import tpu as pltpu
from jax.sharding import PartitionSpec as P

very_negative = -1e30


def moved_to(block, target):
    count_cols = lax.axis_size("col")
    pairs = []
    for p in range(lax.axis_size("pb")):
        for c in range(count_cols):
            q, d = target(p, c)
            pairs.append((p * count_cols + c, q * count_cols + d))
    return lax.ppermute(block, ("pb", "col"), pairs)


def swapped(block, bits):
    return moved_to(block, lambda p, c: (p, c ^ bits))


def softmax_cols(blocks):
    top = functools.reduce(jnp.maximum, [jnp.max(block, axis=0, keepdims=True) for block in blocks])
    blocks = [jnp.exp(block - top) for block in blocks]
    total = functools.reduce(jnp.add, [jnp.sum(block, axis=0, keepdims=True) for block in blocks])
    scale = 1.0 / total
    return [block * scale for block in blocks]


def piece_col(number, slot_steps, count_cols, own_rows):
    slot, offset = divmod(number, count_cols)
    own_step = slot_steps(lax.axis_index("pb"))[slot]
    own_col = lax.axis_index("col")
    return pl.multiple_of((own_step * count_cols + (own_col ^ offset)) * own_rows, own_rows)


def target_kernel(slot_steps, count_cols, own_rows, mask_ref, packed_ref, target_ref, flat_ref):
    window, count_rows = target_ref.shape
    width = packed_ref.shape[1] - window
    tiles, tile_count = mask_ref.shape
    tile_rows, tile_cols = count_rows // tiles, window // tile_count
    for tile in range(tiles):
        rows = slice(tile * tile_rows, (tile + 1) * tile_rows)
        taught = packed_ref[rows, width:].astype(jnp.float32).T
        lives, blocks = [], []
        for col in range(tile_count):
            part = taught[col * tile_cols : (col + 1) * tile_cols, :]
            live = jnp.broadcast_to(mask_ref[tile : tile + 1, col : col + 1], part.shape) > 0
            lives.append(live)
            blocks.append(jnp.where(live, part, very_negative))
        for col, block in enumerate(softmax_cols(blocks)):
            flat_ref[col * tile_cols : (col + 1) * tile_cols, :] = jnp.where(lives[col], block, -1.0)
        for number in range(window // own_rows):
            col = piece_col(number, slot_steps, count_cols, own_rows)
            target_ref[number * own_rows : (number + 1) * own_rows, rows] = flat_ref[pl.ds(col, own_rows), :]


def grads_kernel(score_scale, places, packed_ref, target_ref, weights_ref, *refs):
    grads_ref, window_ref, send_ref, keep_ref, scores_ref = refs[-5:]
    pieces = refs[:-5]
    own_rows, width = pieces[0].shape[1:]
    count_rows = grads_ref.shape[1]
    lanes = count_rows
    slots, halves = send_ref.shape[:2]
    for number in range(slots * 2 * halves):
        slot, offset = divmod(number, 2 * halves)
        index, place = places[slot]
        window_ref[number * own_rows : (number + 1) * own_rows, :] = pieces[index + offset % 2][place + offset // 2]
    scores_ref[...] = score_scale * lax.dot_general(
        window_ref[...],
        packed_ref[:count_rows, :width],
        (((1,), (1,)), ((), ())),
        preferred_element_type=jnp.float32,
    )
    for first in range(0, count_rows, lanes):
        rows = slice(first, first + lanes)
        target = target_ref[:, rows]
        (student,) = softmax_cols([jnp.where(target >= 0, scores_ref[:, rows], very_negative)])
        factor = weights_ref[:, rows] * score_scale
        grads_ref[:, rows] = (factor * (student - jnp.maximum(target, 0.0))).astype(jnp.bfloat16)
    panel = 2 * halves * own_rows
    for slot in reversed(range(slots)):
        term = jnp.dot(
            grads_ref[slot * panel : (slot + 1) * panel, :],
            packed_ref[:count_rows, :width],
            preferred_element_type=jnp.float32,
        ).astype(jnp.bfloat16)
        for half in range(halves):
            keep_ref[slot, half] = term[2 * half * own_rows : (2 * half + 1) * own_rows, :]
            send_ref[slot, half] = term[(2 * half + 1) * own_rows : (2 * half + 2) * own_rows, :]


def query_grad_kernel(grads_ref, window_ref, out_ref, part_ref, sems):
    count_rows = out_ref.shape[0]
    rows = part_ref.shape[1]
    copies = []
    for tile in range(count_rows // rows):
        part_ref[tile] = lax.dot_general(
            grads_ref[:, tile * rows : (tile + 1) * rows],
            window_ref[...],
            (((0,), (0,)), ((), ())),
            preferred_element_type=jnp.float32,
        )
        copy = pltpu.make_async_copy(
            part_ref.at[tile], out_ref.at[tile * rows : (tile + 1) * rows, :], sems.at[tile]
        )
        copy.start()
        copies.append(copy)
    for copy in copies:
        copy.wait()


def on_device(queries, groups, teacher, tile_mask, weights):
    count_rows, width = queries.shape
    score_scale = 2.0 / math.sqrt(width)
    own_rows = groups.shape[0]
    count_pb, count_cols = lax.axis_size("pb"), lax.axis_size("col")
    window = teacher.shape[1]
    steps = window // (own_rows * count_cols)
    tiles = tile_mask.shape[0]
    evens = range(0, count_cols, 2)
    vmem = pl.BlockSpec(memory_space=pltpu.VMEM)
    far = pl.BlockSpec(memory_space=pltpu.HBM)
    budget = 8 * 2**20 + 6 * window * width * 2 + 2 * count_rows * (window + width) * 4
    params = pltpu.CompilerParams(vmem_limit_bytes=min(budget, 50 * 2**20))

    def slot_steps(p):
        return (0, 2, 3 - 2 * (p % 2), 1 + 2 * (p % 2))

    def own(offset):
        return lambda p, c: (p, c ^ offset)

    def ahead(offset):
        return lambda p, c: ((p + 2) % count_pb, c ^ offset)

    def across(offset):
        return lambda p, c: ((p + 1 + 2 * (p % 2)) % count_pb, c ^ offset)

    def slant(offset):
        return lambda p, c: ((p + 3 - 2 * (p % 2)) % count_pb, c ^ offset)

    def beside(p, c):
        return (p ^ 1, c)

    def reverse(move):
        back = {move(p, c): (p, c) for p in range(count_pb) for c in range(count_cols)}
        return lambda p, c: back[(p, c)]

    def after(value, *others):
        return lax.optimization_barrier((value, *others))[0]

    seconds = [moved_to(groups, ahead(offset)) for offset in evens]
    third = moved_to(groups, across(0))
    packed = jnp.concatenate(
        [
            jnp.concatenate([queries, teacher], axis=1),
            jnp.pad(groups, ((0, 0), (0, window))),
        ],
        axis=0,
    )
    seconds = [after(seconds[0], packed)] + seconds[1:]
    fourths = [moved_to(block, beside) for block in seconds]
    late_packed = after(packed, fourths[0])
    target = pl.pallas_call(
        functools.partial(target_kernel, slot_steps, count_cols, own_rows),
        out_shape=jax.ShapeDtypeStruct((window, count_rows), jnp.float32),
        in_specs=[vmem, vmem],
        out_specs=vmem,
        scratch_shapes=[pltpu.VMEM((window, count_rows // tiles), jnp.float32)],
        compiler_params=params,
        cost_estimate=pl.CostEstimate(
            flops=8 * count_rows * window,
            bytes_accessed=6 * count_rows * window,
            transcendentals=count_rows * window,
        ),
    )(tile_mask, late_packed)
    near_groups = after(groups, seconds[0])
    firsts = [near_groups] + [moved_to(near_groups, own(offset)) for offset in evens[1:]]
    thirds = [third] + [moved_to(third, own(offset)) for offset in evens[1:]]
    blocks = (firsts, seconds, thirds, fourths)
    pieces, places = [], {}
    for together in ((0, 1), (2, 3)):
        block = jnp.stack([part for slot in together for part in blocks[slot]])
        for place, slot in enumerate(together):
            places[slot] = (len(pieces), place * len(evens))
        pieces += [block, moved_to(block, own(1))]

    grads, gathered, send, keep = pl.pallas_call(
        functools.partial(grads_kernel, score_scale, places),
        out_shape=(
            jax.ShapeDtypeStruct((window, count_rows), jnp.bfloat16),
            jax.ShapeDtypeStruct((window, width), jnp.bfloat16),
            jax.ShapeDtypeStruct((steps, count_cols // 2, own_rows, width), jnp.bfloat16),
            jax.ShapeDtypeStruct((steps, count_cols // 2, own_rows, width), jnp.bfloat16),
        ),
        in_specs=[vmem] * (3 + len(pieces)),
        out_specs=(vmem,) * 4,
        scratch_shapes=[pltpu.VMEM((window, count_rows), jnp.float32)],
        compiler_params=params,
        cost_estimate=pl.CostEstimate(
            flops=4 * count_rows * window * width,
            bytes_accessed=2 * count_rows * width + 4 * window * width + 6 * count_rows * window,
            transcendentals=count_rows * window,
        ),
    )(packed, target, weights[None, :], *pieces)

    rows = count_rows // tiles
    query_grad = pl.pallas_call(
        query_grad_kernel,
        out_shape=jax.ShapeDtypeStruct((count_rows, width), jnp.float32),
        in_specs=[vmem, vmem],
        out_specs=far,
        scratch_shapes=[
            pltpu.VMEM((tiles, rows, width), jnp.float32),
            pltpu.SemaphoreType.DMA((tiles,)),
        ],
        compiler_params=params,
        cost_estimate=pl.CostEstimate(
            flops=2 * count_rows * window * width,
            bytes_accessed=4 * count_rows * width + 2 * window * width + 2 * count_rows * window,
            transcendentals=0,
        ),
    )(grads, gathered)

    def arrived(block, move):
        return moved_to(block.astype(jnp.bfloat16), move).astype(jnp.float32)

    sums = {}
    last = None
    for slot in (3, 2, 1, 0):
        other = moved_to(send[slot], own(1))
        if last is not None:
            other = after(other, last)
        last = keep[slot].astype(jnp.float32) + other.astype(jnp.float32)
        sums[slot] = [last[offset // 2] for offset in evens]
    third = sums[2][0]
    for offset in evens[1:]:
        third = third + arrived(sums[2][offset // 2], own(offset))
    group_grad = sums[0][0]
    group_grad = group_grad + arrived(third, reverse(across(0)))
    for offset in evens[1:]:
        group_grad = group_grad + arrived(sums[0][offset // 2], own(offset))
    group_grad = group_grad + arrived(sums[1][0], reverse(ahead(0)))
    for offset in evens[1:]:
        group_grad = group_grad + arrived(sums[1][offset // 2], reverse(ahead(offset)))
    group_grad = group_grad + arrived(sums[3][0], reverse(slant(0)))
    for offset in evens[1:]:
        group_grad = group_grad + arrived(sums[3][offset // 2], reverse(slant(offset)))
    return (query_grad, group_grad)


def solution(mesh):
    placed = (
        P(("pb", "col"), None),
        P(("pb", "col"), None),
        P(("pb", "col"), None),
        P(("pb", "col"), None),
        P(("pb", "col")),
    )
    return jax.shard_map(
        on_device,
        mesh=mesh,
        in_specs=placed,
        out_specs=(P(("pb", "col"), None), P(("pb", "col"), None)),
        check_vma=False,
    )
```

```python
import functools
import math

import jax
import jax.numpy as jnp
from jax import lax
from jax.experimental import pallas as pl
from jax.experimental.pallas import tpu as pltpu
from jax.sharding import PartitionSpec as P

very_negative = -1e30


def moved_to(block, target):
    count_cols = lax.axis_size("col")
    pairs = []
    for p in range(lax.axis_size("pb")):
        for c in range(count_cols):
            q, d = target(p, c)
            pairs.append((p * count_cols + c, q * count_cols + d))
    return lax.ppermute(block, ("pb", "col"), pairs)


def swapped(block, bits):
    return moved_to(block, lambda p, c: (p, c ^ bits))


def softmax_cols(blocks):
    top = functools.reduce(jnp.maximum, [jnp.max(block, axis=0, keepdims=True) for block in blocks])
    blocks = [jnp.exp(block - top) for block in blocks]
    total = functools.reduce(jnp.add, [jnp.sum(block, axis=0, keepdims=True) for block in blocks])
    scale = 1.0 / total
    return [block * scale for block in blocks]


def piece_col(number, slot_steps, count_cols, own_rows):
    slot, offset = divmod(number, count_cols)
    own_step = slot_steps(lax.axis_index("pb"))[slot]
    own_col = lax.axis_index("col")
    return pl.multiple_of((own_step * count_cols + (own_col ^ offset)) * own_rows, own_rows)


def target_kernel(slot_steps, count_cols, own_rows, mask_ref, packed_ref, target_ref, flat_ref):
    window, count_rows = target_ref.shape
    width = packed_ref.shape[1] - window
    tiles, tile_count = mask_ref.shape
    tile_rows, tile_cols = count_rows // tiles, window // tile_count
    for tile in range(tiles):
        rows = slice(tile * tile_rows, (tile + 1) * tile_rows)
        taught = packed_ref[rows, width:].astype(jnp.float32).T
        lives, blocks = [], []
        for col in range(tile_count):
            part = taught[col * tile_cols : (col + 1) * tile_cols, :]
            live = jnp.broadcast_to(mask_ref[tile : tile + 1, col : col + 1], part.shape) > 0
            lives.append(live)
            blocks.append(jnp.where(live, part, very_negative))
        for col, block in enumerate(softmax_cols(blocks)):
            flat_ref[col * tile_cols : (col + 1) * tile_cols, :] = jnp.where(lives[col], block, -1.0)
        for number in range(window // own_rows):
            col = piece_col(number, slot_steps, count_cols, own_rows)
            target_ref[number * own_rows : (number + 1) * own_rows, rows] = flat_ref[pl.ds(col, own_rows), :]


def grads_kernel(score_scale, places, packed_ref, target_ref, weights_ref, *refs):
    grads_ref, window_ref, send_ref, keep_ref, scores_ref = refs[-5:]
    pieces = refs[:-5]
    own_rows, width = pieces[0].shape[1:]
    count_rows = grads_ref.shape[1]
    lanes = count_rows
    slots, halves = send_ref.shape[:2]
    for number in range(slots * 2 * halves):
        slot, offset = divmod(number, 2 * halves)
        index, place = places[slot]
        window_ref[number * own_rows : (number + 1) * own_rows, :] = pieces[index + offset % 2][place + offset // 2]
    scores_ref[...] = score_scale * lax.dot_general(
        window_ref[...],
        packed_ref[:count_rows, :width],
        (((1,), (1,)), ((), ())),
        preferred_element_type=jnp.float32,
    )
    for first in range(0, count_rows, lanes):
        rows = slice(first, first + lanes)
        target = target_ref[:, rows]
        (student,) = softmax_cols([jnp.where(target >= 0, scores_ref[:, rows], very_negative)])
        factor = weights_ref[:, rows] * score_scale
        grads_ref[:, rows] = (factor * (student - jnp.maximum(target, 0.0))).astype(jnp.bfloat16)
    panel = 2 * halves * own_rows
    for slot in reversed(range(slots)):
        term = jnp.dot(
            grads_ref[slot * panel : (slot + 1) * panel, :],
            packed_ref[:count_rows, :width],
            preferred_element_type=jnp.float32,
        ).astype(jnp.bfloat16)
        for half in range(halves):
            keep_ref[slot, half] = term[2 * half * own_rows : (2 * half + 1) * own_rows, :]
            send_ref[slot, half] = term[(2 * half + 1) * own_rows : (2 * half + 2) * own_rows, :]


def query_grad_kernel(grads_ref, window_ref, out_ref, part_ref, sems):
    count_rows = out_ref.shape[0]
    rows = part_ref.shape[1]
    copies = []
    for tile in range(count_rows // rows):
        part_ref[tile] = lax.dot_general(
            grads_ref[:, tile * rows : (tile + 1) * rows],
            window_ref[...],
            (((0,), (0,)), ((), ())),
            preferred_element_type=jnp.float32,
        )
        copy = pltpu.make_async_copy(
            part_ref.at[tile], out_ref.at[tile * rows : (tile + 1) * rows, :], sems.at[tile]
        )
        copy.start()
        copies.append(copy)
    for copy in copies:
        copy.wait()


def on_device(queries, groups, teacher, tile_mask, weights):
    count_rows, width = queries.shape
    score_scale = 2.0 / math.sqrt(width)
    own_rows = groups.shape[0]
    count_pb, count_cols = lax.axis_size("pb"), lax.axis_size("col")
    window = teacher.shape[1]
    steps = window // (own_rows * count_cols)
    tiles = tile_mask.shape[0]
    evens = range(0, count_cols, 2)
    vmem = pl.BlockSpec(memory_space=pltpu.VMEM)
    far = pl.BlockSpec(memory_space=pltpu.HBM)
    budget = 8 * 2**20 + 6 * window * width * 2 + 2 * count_rows * (window + width) * 4
    params = pltpu.CompilerParams(vmem_limit_bytes=min(budget, 50 * 2**20))

    def slot_steps(p):
        return (0, 2, 3 - 2 * (p % 2), 1 + 2 * (p % 2))

    def own(offset):
        return lambda p, c: (p, c ^ offset)

    def ahead(offset):
        return lambda p, c: ((p + 2) % count_pb, c ^ offset)

    def across(offset):
        return lambda p, c: ((p + 1 + 2 * (p % 2)) % count_pb, c ^ offset)

    def slant(offset):
        return lambda p, c: ((p + 3 - 2 * (p % 2)) % count_pb, c ^ offset)

    def beside(p, c):
        return (p ^ 1, c)

    def reverse(move):
        back = {move(p, c): (p, c) for p in range(count_pb) for c in range(count_cols)}
        return lambda p, c: back[(p, c)]

    def after(value, *others):
        return lax.optimization_barrier((value, *others))[0]

    seconds = [moved_to(groups, ahead(offset)) for offset in evens]
    third = moved_to(groups, across(0))
    packed = jnp.concatenate(
        [
            jnp.concatenate([queries, teacher], axis=1),
            jnp.pad(groups, ((0, 0), (0, window))),
        ],
        axis=0,
    )
    seconds = [after(seconds[0], packed)] + seconds[1:]
    fourths = [moved_to(block, beside) for block in seconds]
    late_packed = after(packed, fourths[0])
    target = pl.pallas_call(
        functools.partial(target_kernel, slot_steps, count_cols, own_rows),
        out_shape=jax.ShapeDtypeStruct((window, count_rows), jnp.float32),
        in_specs=[vmem, vmem],
        out_specs=vmem,
        scratch_shapes=[pltpu.VMEM((window, count_rows // tiles), jnp.float32)],
        compiler_params=params,
        cost_estimate=pl.CostEstimate(
            flops=8 * count_rows * window,
            bytes_accessed=6 * count_rows * window,
            transcendentals=count_rows * window,
        ),
    )(tile_mask, late_packed)
    near_groups = after(groups, seconds[0])
    firsts = [near_groups] + [moved_to(near_groups, own(offset)) for offset in evens[1:]]
    thirds = [third] + [moved_to(third, own(offset)) for offset in evens[1:]]
    blocks = (firsts, seconds, thirds, fourths)
    pieces, places = [], {}
    for together in ((0, 1), (2, 3)):
        block = jnp.stack([part for slot in together for part in blocks[slot]])
        for place, slot in enumerate(together):
            places[slot] = (len(pieces), place * len(evens))
        pieces += [block, moved_to(block, own(1))]

    grads, gathered, send, keep = pl.pallas_call(
        functools.partial(grads_kernel, score_scale, places),
        out_shape=(
            jax.ShapeDtypeStruct((window, count_rows), jnp.bfloat16),
            jax.ShapeDtypeStruct((window, width), jnp.bfloat16),
            jax.ShapeDtypeStruct((steps, count_cols // 2, own_rows, width), jnp.bfloat16),
            jax.ShapeDtypeStruct((steps, count_cols // 2, own_rows, width), jnp.bfloat16),
        ),
        in_specs=[vmem] * (3 + len(pieces)),
        out_specs=(vmem,) * 4,
        scratch_shapes=[pltpu.VMEM((window, count_rows), jnp.float32)],
        compiler_params=params,
        cost_estimate=pl.CostEstimate(
            flops=4 * count_rows * window * width,
            bytes_accessed=2 * count_rows * width + 4 * window * width + 6 * count_rows * window,
            transcendentals=count_rows * window,
        ),
    )(packed, target, weights[None, :], *pieces)

    rows = count_rows // tiles
    query_grad = pl.pallas_call(
        query_grad_kernel,
        out_shape=jax.ShapeDtypeStruct((count_rows, width), jnp.float32),
        in_specs=[vmem, vmem],
        out_specs=far,
        scratch_shapes=[
            pltpu.VMEM((tiles, rows, width), jnp.float32),
            pltpu.SemaphoreType.DMA((tiles,)),
        ],
        compiler_params=params,
        cost_estimate=pl.CostEstimate(
            flops=2 * count_rows * window * width,
            bytes_accessed=4 * count_rows * width + 2 * window * width + 2 * count_rows * window,
            transcendentals=0,
        ),
    )(grads, gathered)

    def arrived(block, move):
        return moved_to(block.astype(jnp.bfloat16), move).astype(jnp.float32)

    sums = {}
    last = None
    for slot in (2, 0, 3, 1):
        other = moved_to(send[slot], own(1))
        if last is not None:
            other = after(other, last)
        last = keep[slot].astype(jnp.float32) + other.astype(jnp.float32)
        sums[slot] = [last[offset // 2] for offset in evens]
    third = sums[2][0]
    for offset in evens[1:]:
        third = third + arrived(sums[2][offset // 2], own(offset))
    sums[1][1:] = [after(block, third) for block in sums[1][1:]]
    group_grad = sums[0][0]
    group_grad = group_grad + arrived(third, reverse(across(0)))
    group_grad = group_grad + arrived(sums[3][0], reverse(slant(0)))
    for offset in evens[1:]:
        group_grad = group_grad + arrived(sums[3][offset // 2], reverse(slant(offset)))
    group_grad = group_grad + arrived(sums[1][0], reverse(ahead(0)))
    for offset in evens[1:]:
        group_grad = group_grad + arrived(sums[1][offset // 2], reverse(ahead(offset)))
    for offset in evens[1:]:
        group_grad = group_grad + arrived(sums[0][offset // 2], own(offset))
    return (query_grad, group_grad)


def solution(mesh):
    placed = (
        P(("pb", "col"), None),
        P(("pb", "col"), None),
        P(("pb", "col"), None),
        P(("pb", "col"), None),
        P(("pb", "col")),
    )
    return jax.shard_map(
        on_device,
        mesh=mesh,
        in_specs=placed,
        out_specs=(P(("pb", "col"), None), P(("pb", "col"), None)),
        check_vma=False,
    )
```
